128 devices in a mesh: row: 8 (over y, x_hi), col: 16 (over z, x_lo, core).
Axes of the slice: x: 4 (x_hi: 2, x_lo: 2; x = x_hi * 2 + x_lo), y: 4, z: 4, core: 2. Of those that a mesh axis runs over, the one named last changes fastest.
Arguments:
- amplitudes: float32 [384, 384, 1600], P('row', 'col'), may hold values from -6 to 6
- hole_ladder: float32 [1600, 1600], P('col'), may hold values from -0.15625 to 0.15625
- e_occ: float32 [40], replicated, may hold values from -2 to -0.5
- e_vir: float32 [384], replicated, may hold values from 0.5 to 4
- ladder_ints: float32 [384, 384, 256], P('col'), may hold values from -0.09375 to 0.09375
- pair_group: int32 [820], replicated, may hold values from 0 to 7, as said below
Outputs:
- new_amplitudes: float32 [8, 205, 384, 384], P('row', None, 'col')
- particle_term: float32 [8, 256, 205], P('row', 'col')
The draws below stay inside these ranges and needn't reach their ends.
Inputs may be any that keep to these rules, and one draw needn't show every extreme that they name: `pair_group`: each pair names its row group; no group holds more than 205 pairs, and one group holds exactly 205.
All inputs are finite; a program needn't handle non-finite values.
Results may differ from the reference program's by a relative error of at most 0.00011.
Values sent between devices are 32-bit elements; how exact they have to be, the bound alone decides.
No kernel may reach another device: no remote copies, remote signals or barrier semaphores. Data moves between devices by JAX's collectives and lax.ppermute only.
A program may use at most 192 MiB of HBM per device.

```python
import jax
import jax.numpy as jnp
import numpy as np
from jax import lax

O = 40
V = 384
AB_WIN = 256
P_SIZE = 1600
PAIRS = 820
GROUPS = 8
CAP = 205


def draw_pair_group(key, part):
    key = jax.random.fold_in(key, 11)
    hot_key, order_key, spread_key = jax.random.split(key, 3)
    hottest = jax.random.randint(hot_key, (), 0, GROUPS)
    shuffled = jax.random.permutation(order_key, PAIRS)
    position = jnp.argsort(shuffled)
    spare = PAIRS - CAP
    scattered = spare // 6
    even_part = spare - scattered
    others = max(GROUPS - 1, 1)
    ordered_other = (position - CAP) % others
    random_other = jax.random.randint(spread_key, (PAIRS,), 0, others)
    other_rank = jnp.where(position < CAP + even_part, ordered_other, random_other)
    group_ids = jnp.where(position < CAP, hottest, (hottest + 1 + other_rank) % GROUPS)
    return group_ids.astype(jnp.int32)


def strengthened(entries, key, source, target, shards_of, factor):
    owner, partner = [(jnp.arange(entries.shape[axis_at]) // (entries.shape[axis_at] // shards_of)).reshape([-1 if axis == axis_at else 1 for axis in range(entries.ndim)]) for axis_at in (source, target)]
    chosen = jax.random.permutation(key, shards_of)[partner]
    strong = (owner == chosen) | (owner == (partner + shards_of // 2) % shards_of)
    return jnp.where(strong, factor * entries, entries)


def block_levels(stream_key, shape, shards, low, largest):
    def one(dim, shards_of):
        heights = jax.random.uniform(jax.random.fold_in(jax.random.fold_in(stream_key, 6), dim), (shards_of,), jnp.float32, low / len(shards), largest / len(shards))
        return jnp.repeat(jnp.exp(heights), shape[dim] // shards_of).reshape((-1,) + (1,) * (len(shape) - dim - 1))

    factor_of = one(*shards[0])
    for cut in shards[1:]:
        factor_of = factor_of * one(*cut)
    return factor_of


def normal_values(own_key, extent, deviation, reach, shards=(), kind=jnp.bfloat16):
    entries = jax.random.normal(own_key, extent, jnp.float32) * deviation
    if len(shards) > 0:
        entries = block_levels(own_key, extent, shards, -0.22, 0.18) * entries
    return jnp.clip(entries, min=-reach, max=reach).astype(kind)


def noise_with(key, dims, scale, limit, cuts, heavy, held_as=jnp.bfloat16):
    result = scale * jax.random.normal(key, dims, jnp.float32)
    if cuts:
        result = result * block_levels(key, dims, cuts, -0.22, 0.18)
    return jnp.clip(strengthened(result, jax.random.fold_in(key, 3), *heavy), -limit, limit).astype(held_as)


def setup_inputs(seed: int = 0) -> dict:
    splits = jax.random.split(jax.random.key(seed), 7)
    amplitudes = normal_values(splits[0], (V, V, P_SIZE), 1.0, 6.0, ((0, 8), (1, 16)), jnp.float32)
    hole_ladder = normal_values(splits[1], (P_SIZE, P_SIZE), P_SIZE ** -0.5, 0.15625, ((0, 16),), jnp.float32)
    e_occ = jnp.clip(jax.random.uniform(splits[2], (O,), jnp.float32, -2.0, -0.5), -2.0, -0.5)
    e_vir = jnp.clip(jax.random.uniform(splits[3], (V,), jnp.float32, 0.5, 4.0), 0.5, 4.0)
    ladder_ints = noise_with(splits[4], (V, V, AB_WIN), (V * V // 16) ** -0.5, 0.09375, ((0, 16),), (0, 2, 16, 2.0), jnp.float32)
    pair_group = draw_pair_group(jax.random.fold_in(splits[6], 71), 0)
    return {"amplitudes": amplitudes, "hole_ladder": hole_ladder, "e_occ": e_occ, "e_vir": e_vir, "ladder_ints": ladder_ints, "pair_group": pair_group}


def build_slots(pair_group, groups, capacity, occ_count):
    pair_count = pair_group.shape[0]
    upper_rows, upper_cols = np.triu_indices(occ_count)
    onehot = (pair_group[:, None] == jnp.arange(groups, dtype=jnp.int32)[None, :]).astype(jnp.int32)
    slot_index = jnp.sum(jnp.cumsum(onehot, axis=0) * onehot, axis=1) - 1
    slot_table = jnp.full((groups, capacity), pair_count, jnp.int32)
    slot_table = slot_table.at[pair_group, slot_index].set(jnp.arange(pair_count, dtype=jnp.int32))
    live_mask = slot_table < pair_count
    safe_index = jnp.where(live_mask, slot_table, 0)
    first_occ = jnp.asarray(upper_rows, jnp.int32)[safe_index]
    second = jnp.asarray(upper_cols, jnp.int32)[safe_index]
    return live_mask, first_occ, second


def reference(amplitudes, hole_ladder, e_occ, e_vir, ladder_ints, pair_group):
    live_mask, first_occ, second = build_slots(pair_group, GROUPS, CAP, O)
    flat_amps = amplitudes.reshape(V * V, O * O)
    flat_ints = ladder_ints.reshape(V * V, AB_WIN)

    def per_group(group_index):
        own_first = first_occ[group_index]
        own_second = second[group_index]
        direct_cols = own_first * O + own_second
        swap_cols = own_second * O + own_first
        direct = jnp.dot(flat_amps, hole_ladder[:, direct_cols], precision=lax.Precision.HIGHEST, preferred_element_type=jnp.float32).reshape(V, V, CAP)
        swapped = jnp.dot(flat_amps, hole_ladder[:, swap_cols], precision=lax.Precision.HIGHEST, preferred_element_type=jnp.float32).reshape(V, V, CAP)
        summed = direct + jnp.transpose(swapped, (1, 0, 2))
        denominator = (e_occ[own_first] + e_occ[own_second])[None, None, :] - e_vir[:, None, None] - e_vir[None, :, None]
        group_amps = jnp.where(live_mask[group_index][None, None, :], summed / denominator, jnp.float32(0.0))
        ordered = jnp.transpose(group_amps, (2, 1, 0))
        ladder = jnp.dot(ordered.reshape(CAP, V * V), flat_ints, precision=lax.Precision.HIGHEST, preferred_element_type=jnp.float32)
        return ordered, jnp.transpose(ladder, (1, 0))

    group_amps, ladder = lax.map(per_group, jnp.arange(GROUPS, dtype=jnp.int32))
    return group_amps, ladder
```

```python
import functools

import jax
import jax.numpy as jnp
import numpy as np
from jax import lax
from jax.experimental import pallas as pl
from jax.experimental.pallas import tpu as pltpu
from jax.sharding import PartitionSpec as P

F32 = jnp.float32
BF16 = jnp.bfloat16
BINS = 8
SLOTS = 104
ALL_SLOTS = BINS * SLOTS
SPILL = 20
PAIR_PAD = 896
GROUP_SLOTS = 256
OCC = 40
VMEM_LIMIT = 56 * 1024 * 1024


def split2(x):
    hi = x.astype(BF16)
    return hi, (x - hi.astype(F32)).astype(BF16)


def split3(x):
    hi = x.astype(BF16)
    rest = x - hi.astype(F32)
    mid = rest.astype(BF16)
    return hi, mid, (rest - mid.astype(F32)).astype(BF16)


def dot(a, b):
    return jnp.dot(a, b, preferred_element_type=F32)


def dot_t(a, b):
    return lax.dot_general(a, b, (((1,), (1,)), ((), ())), preferred_element_type=F32)


def iota(shape, dim):
    return lax.broadcasted_iota(jnp.int32, shape, dim)


def prep_kernel(own_ref, group_ref, occ_ref, eocc_ref, w_ref, mirror_out, direct_out, slot_out, group_out, bin_out):
    group = group_ref[...]
    onehot = jnp.where(group == iota((BINS, PAIR_PAD), 0), 1.0, 0.0)
    before = jnp.where(iota((PAIR_PAD, PAIR_PAD), 0) < iota((PAIR_PAD, PAIR_PAD), 1), 1.0, 0.0).astype(BF16)
    rank = jnp.sum(dot(onehot.astype(BF16), before) * onehot, axis=0, keepdims=True)
    valid = jnp.sum(onehot, axis=0, keepdims=True)
    count = jnp.sum(onehot, axis=1, keepdims=True)
    kept = jnp.minimum(count, float(SLOTS))
    spilled = jnp.where(rank >= float(SLOTS), valid, 0.0)
    order = dot(jnp.broadcast_to(spilled, (BINS, PAIR_PAD)).astype(BF16), before)
    total = jnp.sum(spilled, axis=1, keepdims=True)
    free = float(SLOTS) - kept
    short = jnp.minimum(free, float(SPILL))
    fits = jnp.sum(short, axis=0, keepdims=True) >= total
    room = jnp.where(fits, short, free)
    bin_row = iota((BINS, 1), 0)
    first = jnp.zeros((BINS, 1), F32)
    for b in range(BINS - 1):
        first = first + jnp.where(bin_row > b, room[b : b + 1, :], 0.0)
    inside = jnp.where(order >= first, jnp.where(order < first + room, 1.0, 0.0), 0.0)
    is_spilled = spilled > 0.5
    bin_hot = jnp.where(is_spilled, inside, onehot)
    bin_of = jnp.sum(bin_hot * bin_row.astype(F32), axis=0, keepdims=True)
    moved = jnp.sum(inside * (kept - first), axis=0, keepdims=True) + order[0:1, :]
    slot_of = jnp.where(is_spilled, moved, rank)
    place = jnp.where(valid > 0.5, bin_of * float(SLOTS) + slot_of, -1.0)
    own_rank = jnp.where(group == own_ref[0], rank, -1.0)
    stack = jnp.concatenate([place, own_rank, jnp.zeros((6, PAIR_PAD), F32)], axis=0)
    columns = jnp.transpose(stack, (1, 0))
    place_col = columns[:, 0:1].astype(jnp.int32)
    rank_col = columns[:, 1:2].astype(jnp.int32)
    to_slot = jnp.where(place_col == iota((PAIR_PAD, ALL_SLOTS), 1), 1.0, 0.0).astype(BF16)
    slots = dot(occ_ref[...].astype(BF16), to_slot)
    slot_i, slot_j, live = slots[0:1, :], slots[1:2, :], slots[2:3, :]
    occ_row = iota((OCC, 1), 0).astype(F32)
    energy = jnp.sum(
        jnp.where(slot_i == occ_row, eocc_ref[...], 0.0), axis=0, keepdims=True
    ) + jnp.sum(jnp.where(slot_j == occ_row, eocc_ref[...], 0.0), axis=0, keepdims=True)
    slot_out[...] = jnp.concatenate([energy, live, jnp.zeros((6, ALL_SLOTS), F32)], axis=0)
    to_group = jnp.where(rank_col == iota((PAIR_PAD, GROUP_SLOTS), 1), 1.0, 0.0).astype(BF16)
    source = jnp.concatenate([bin_of, slot_of, valid, jnp.zeros((5, PAIR_PAD), F32)], axis=0)
    group_out[...] = dot(source.astype(BF16), to_group).astype(jnp.int32)
    taken = jnp.minimum(jnp.maximum(total - first, 0.0), room)
    bin_cols = jnp.concatenate([count, kept, first, taken, jnp.zeros((BINS, 124), F32)], axis=1)
    bin_out[...] = bin_cols.astype(jnp.int32)

    parts = split3(w_ref[...])
    rows = w_ref.shape[0]
    for left, right, w_out in ((slot_j, slot_i, mirror_out), (slot_i, slot_j, direct_out)):
        wanted = jnp.where(live > 0.5, left * float(OCC) + right, -1.0).astype(jnp.int32)
        w_out[...] = jnp.zeros(w_out.shape, F32)
        for lane in range(0, ALL_SLOTS, 128):
            wide = min(128, ALL_SLOTS - lane)
            pick = jnp.where(
                iota((OCC * OCC, wide), 0) == wanted[:, lane : lane + wide], 1.0, 0.0
            ).astype(BF16)
            w_out[0:rows, lane : lane + wide] = (dot(parts[0], pick) + dot(parts[1], pick)) + dot(
                parts[2], pick
            )


def prep(own, pair_group, e_occ, hole_ladder):
    pairs = pair_group.shape[0]
    first, second = np.triu_indices(OCC)
    occ = np.zeros((8, PAIR_PAD), np.float32)
    occ[0, :pairs], occ[1, :pairs], occ[2, :pairs] = first, second, 1.0
    group = jnp.pad(pair_group, (0, PAIR_PAD - pairs), constant_values=BINS).reshape(1, PAIR_PAD)
    vmem = pl.BlockSpec(memory_space=pltpu.VMEM)
    return pl.pallas_call(
        prep_kernel,
        out_shape=(
            jax.ShapeDtypeStruct((104, ALL_SLOTS), F32),
            jax.ShapeDtypeStruct((104, ALL_SLOTS), F32),
            jax.ShapeDtypeStruct((8, ALL_SLOTS), F32),
            jax.ShapeDtypeStruct((8, GROUP_SLOTS), jnp.int32),
            jax.ShapeDtypeStruct((BINS, 128), jnp.int32),
        ),
        in_specs=[pl.BlockSpec(memory_space=pltpu.SMEM)] + [vmem] * 4,
        out_specs=(vmem,) * 5,
        compiler_params=pltpu.CompilerParams(vmem_limit_bytes=VMEM_LIMIT),
    )(own, group, jnp.asarray(occ), e_occ.reshape(OCC, 1), hole_ladder)


def tile_kernel(t_ref, mirror_hi, mirror_lo, direct_hi, direct_lo):
    for h in range(2):
        for tile in range(5):
            for q in range(8):
                pieces = []
                for e in (2 * q, 2 * q + 1):
                    unit = 5 * tile + e // 3
                    if e < 15 and unit < 24:
                        pieces.append(t_ref[24 * h + unit, 8 * (e % 3) : 8 * (e % 3) + 8, :])
                    else:
                        pieces.append(jnp.zeros((8, 1600), F32))
                hi, lo = split2(jnp.concatenate(pieces, axis=0))
                at = 640 * h + 128 * tile + 16 * q
                mirror_hi[at : at + 16, :] = hi
                mirror_lo[at : at + 16, :] = lo
    for b in range(24):
        hi, lo = split2(t_ref[:, b, :])
        direct_hi[48 * b : 48 * (b + 1), :] = hi
        direct_lo[48 * b : 48 * (b + 1), :] = lo
    direct_hi[1152:1280, :] = jnp.zeros((128, 1600), BF16)
    direct_lo[1152:1280, :] = jnp.zeros((128, 1600), BF16)


def tile_parts(amplitudes):
    vmem = pl.BlockSpec(memory_space=pltpu.VMEM)
    return pl.pallas_call(
        tile_kernel,
        out_shape=(jax.ShapeDtypeStruct((1280, 1600), BF16),) * 4,
        in_specs=[vmem],
        out_specs=(vmem,) * 4,
        compiler_params=pltpu.CompilerParams(vmem_limit_bytes=VMEM_LIMIT),
        cost_estimate=pl.CostEstimate(flops=0, bytes_accessed=60_000_000, transcendentals=0),
    )(amplitudes)


def hole_kernel(mirror, w_ref, t_hi, t_lo, out_ref, wn, wt_hi, wt_lo):
    for s in range(16):
        wn[100 * s : 100 * s + 100, :] = w_ref[104 * s : 104 * s + 100, :]
    for lane in range(0, ALL_SLOTS, 128):
        wide = min(128, ALL_SLOTS - lane)
        hi, lo = split2(jnp.transpose(wn[:, lane : lane + wide], (1, 0)))
        wt_hi[lane : lane + wide, :] = hi
        wt_lo[lane : lane + wide, :] = lo

    for n in range(5):
        right_hi, right_lo = t_hi[256 * n : 256 * (n + 1), :], t_lo[256 * n : 256 * (n + 1), :]
        y = (dot_t(wt_lo[...], right_hi) + dot_t(wt_hi[...], right_lo)) + dot_t(wt_hi[...], right_hi)
        for b in range(BINS):
            rows = slice(SLOTS * b, SLOTS * (b + 1))
            if mirror:
                for u in range(2):
                    h, lane = divmod(2 * n + u, 5)
                    out_ref[b, h, :, 128 * lane : 128 * (lane + 1)] = y[rows, 128 * u : 128 * (u + 1)]
            else:
                wide = 256 if n < 4 else 128
                out_ref[b, :, 256 * n : 256 * n + wide] = y[rows, 0:wide]


def hole_product(mirror, gathered, hi, lo):
    shape = (BINS, 2, SLOTS, 640) if mirror else (BINS, SLOTS, 1152)
    vmem = pl.BlockSpec(memory_space=pltpu.VMEM)
    return pl.pallas_call(
        functools.partial(hole_kernel, mirror),
        out_shape=jax.ShapeDtypeStruct(shape, F32),
        in_specs=[vmem] * 3,
        out_specs=vmem,
        scratch_shapes=[
            pltpu.VMEM((1600, ALL_SLOTS), F32),
            pltpu.VMEM((ALL_SLOTS, 1600), BF16),
            pltpu.VMEM((ALL_SLOTS, 1600), BF16),
        ],
        compiler_params=pltpu.CompilerParams(vmem_limit_bytes=VMEM_LIMIT),
        cost_estimate=pl.CostEstimate(
            flops=2 * 3 * ALL_SLOTS * 1280 * 1600, bytes_accessed=17_000_000, transcendentals=0
        ),
    )(gathered, hi, lo)


def combine_kernel(meta_ref, ed_ref, d_ref, s_ref, eo_ref, ev_ref, ladder_ref, new_ref, seg_ref, part_ref, m_ref, raw, acc):
    step = pl.program_id(0)
    kept, start = meta_ref[0], meta_ref[1]
    energy = eo_ref[:, 0:1] - ev_ref[...]
    live = eo_ref[:, 1:2] > 0.5
    rest = new_ref.shape[0] - SLOTS

    def group(j):
        for u in range(8):
            d = 8 * j + u
            direct = jnp.concatenate([d_ref[r, :, 48 * u : 48 * (u + 1)] for r in range(8)], axis=1)
            lane = 128 * (d // 5) + 24 * (d % 5)
            mirrored = jnp.concatenate([s_ref[c, :, lane : lane + 24] for c in range(16)], axis=1)
            value = jnp.where(live, (direct + mirrored) / (energy - ed_ref[d]), 0.0)
            m_ref[:, 384 * u : 384 * (u + 1)] = value
            raw[:, u, :] = value

    for j in range(3):
        pl.when(step == j)(functools.partial(group, j))

    new_ref[0:SLOTS] = jnp.where(iota((SLOTS, 8, 384), 0) < kept, raw[...], 0.0)
    new_ref[SLOTS:] = jnp.zeros((rest, 8, 384), F32)
    seg_ref[...] = raw[pl.ds(start, SPILL)]

    left_hi, left_lo = split2(m_ref[...])
    right_hi, right_lo = split2(ladder_ref[...].reshape(8 * 384, 256))
    term = (dot(left_lo, right_hi) + dot(left_hi, right_lo)) + dot(left_hi, right_hi)

    @pl.when(step == 0)
    def _():
        acc[...] = jnp.zeros(acc.shape, F32)

    acc[0:SLOTS, :] += term

    @pl.when(step == 2)
    def _():
        part_ref[...] = jnp.transpose(acc[...], (1, 0))


def combine(meta, ed, direct, mirrored, energy, ev, ladder, rows):
    smem = pl.BlockSpec(memory_space=pltpu.SMEM)
    return pl.pallas_call(
        combine_kernel,
        grid=(3,),
        out_shape=(
            jax.ShapeDtypeStruct((rows, 24, 384), F32),
            jax.ShapeDtypeStruct((SPILL, 24, 384), F32),
            jax.ShapeDtypeStruct((256, 128), F32),
        ),
        in_specs=[
            smem,
            smem,
            pl.BlockSpec((8, SLOTS, 384), lambda j: (0, 0, j)),
            pl.BlockSpec((16, SLOTS, 640), lambda j: (0, 0, 0)),
            pl.BlockSpec((SLOTS, 2), lambda j: (0, 0)),
            pl.BlockSpec((1, 384), lambda j: (0, 0)),
            pl.BlockSpec((8, 384, 256), lambda j: (j, 0, 0)),
        ],
        out_specs=(
            pl.BlockSpec((rows, 8, 384), lambda j: (0, j, 0)),
            pl.BlockSpec((SPILL, 8, 384), lambda j: (0, j, 0)),
            pl.BlockSpec((256, 128), lambda j: (0, 0)),
        ),
        scratch_shapes=[
            pltpu.VMEM((SLOTS, 8 * 384), F32),
            pltpu.VMEM((SLOTS, 8, 384), F32),
            pltpu.VMEM((128, 256), F32),
        ],
        compiler_params=pltpu.CompilerParams(vmem_limit_bytes=VMEM_LIMIT),
        cost_estimate=pl.CostEstimate(
            flops=2 * 3 * 128 * 9216 * 256, bytes_accessed=60_000_000, transcendentals=0
        ),
    )(meta, ed, direct, mirrored, energy, ev, ladder)


def place_kernel(table_ref, new_ref, *refs):
    back_refs, out_ref, sem = refs[:BINS], refs[BINS], refs[BINS + 1]
    for b in range(BINS):

        def send(k, carry, b=b):
            row = back_refs[b].at[table_ref[0, b] + k]
            pltpu.make_async_copy(row, out_ref.at[table_ref[1, b] + k], sem).start()
            return carry

        lax.fori_loop(0, table_ref[2, b], send, 0)

    for b in range(BINS):

        def wait(k, carry, b=b):
            pltpu.make_async_copy(back_refs[b].at[k], out_ref.at[k], sem).wait()
            return carry

        lax.fori_loop(0, table_ref[2, b], wait, 0)


def place(table, new, backs):
    hbm = pl.BlockSpec(memory_space=pl.ANY)
    vmem = pl.BlockSpec(memory_space=pltpu.VMEM)
    return pl.pallas_call(
        place_kernel,
        out_shape=jax.ShapeDtypeStruct(new.shape, F32),
        in_specs=[pl.BlockSpec(memory_space=pltpu.SMEM), hbm] + [vmem] * BINS,
        out_specs=hbm,
        scratch_shapes=[pltpu.SemaphoreType.DMA],
        input_output_aliases={1: 0},
        compiler_params=pltpu.CompilerParams(vmem_limit_bytes=VMEM_LIMIT),
    )(table, new, *backs)


def shards(amplitudes, hole_ladder, e_occ, e_vir, ladder_ints, pair_group):
    tile_cols = amplitudes.shape[1]
    capacity = 2 * pair_group.shape[0] // lax.axis_size("row")
    own = lax.axis_index("row")
    col_index = lax.axis_index("col")

    w_mirror, w_direct, slot_table, group_table, bin_table = prep(
        own.reshape(1), pair_group, e_occ, hole_ladder
    )
    w_mirror = lax.all_gather(w_mirror, "col", axis=0, tiled=True)
    w_direct = lax.all_gather(w_direct, "col", axis=0, tiled=True)
    mirror_hi, mirror_lo, direct_hi, direct_lo = tile_parts(amplitudes)
    mirror_src = hole_product(True, w_mirror, mirror_hi, mirror_lo)
    mirrored = lax.all_to_all(mirror_src, "row", 0, 0).reshape(16, SLOTS, 640)
    direct_src = hole_product(False, w_direct, direct_hi, direct_lo)
    mirrored = lax.all_to_all(mirrored, "col", 0, 0)
    direct = lax.all_to_all(direct_src, "row", 0, 0)

    counts, kept, first, taken = (bin_table[:, k] for k in range(4))
    own_count = lax.dynamic_index_in_dim(counts, own, 0, False)
    own_kept = jnp.minimum(own_count, SLOTS)
    start = jnp.minimum(kept, SLOTS - SPILL)
    own_start = lax.dynamic_index_in_dim(start, own, 0, False)
    energy = lax.dynamic_slice(slot_table, (0, own * SLOTS), (2, SLOTS)).T
    local_energy = lax.dynamic_slice_in_dim(e_vir, col_index * tile_cols, tile_cols)
    virtual = e_vir.reshape(1, -1)
    new_rows, segment, partial_value = combine(
        jnp.stack([own_kept, own_start]), local_energy, direct, mirrored, energy, virtual, ladder_ints, capacity
    )

    blocks = lax.all_to_all(partial_value.reshape(16, 16, 128), "col", 0, 0)
    share = jnp.sum(blocks, axis=0)
    shares = lax.all_to_all(jnp.broadcast_to(share, (BINS, 16, 128)), "row", 0, 0)
    live = group_table[2, :capacity]
    from_bin, from_slot = group_table[0, :capacity], group_table[1, :capacity]
    where_from = jnp.where(live > 0, from_bin * 128 + from_slot, -1)
    pick = jnp.arange(BINS * 128, dtype=jnp.int32)[:, None] == where_from[None, :]
    ladder_share = jnp.dot(
        jnp.transpose(shares, (1, 0, 2)).reshape(16, BINS * 128),
        pick.astype(F32),
        precision=lax.Precision.HIGHEST,
        preferred_element_type=F32,
    )

    hot = jnp.argmax(counts).astype(jnp.int32)
    fits = (jnp.sum((counts > SLOTS).astype(jnp.int32)) <= 1) & (jnp.max(taken) <= SPILL)

    def short_way(h, operands):
        segment = operands[0]
        return tuple(
            segment if r == h else lax.ppermute(segment, "row", [(r, h)]) for r in range(BINS)
        )

    def long_way(operands):
        _, direct, mirrored = operands
        whole = jnp.stack([jnp.int32(SLOTS), jnp.int32(0)])
        values, _, _ = combine(
            whole, local_energy, direct, mirrored, energy, virtual, ladder_ints, capacity
        )
        everything = lax.all_gather(values[:SLOTS], "row", axis=0, tiled=True)
        index = jnp.pad((from_bin * SLOTS + from_slot)[SLOTS:], (0, BINS * SPILL + SLOTS - capacity))
        late = everything[index].reshape(BINS, SPILL, 24, 384)
        return tuple(late[b] for b in range(BINS))

    ways = [functools.partial(short_way, h) for h in range(BINS)] + [long_way]
    backs = lax.switch(jnp.where(fits, hot, BINS), ways, (segment, direct, mirrored))
    late_count = own_count - own_kept
    bins = SPILL * jnp.arange(BINS, dtype=jnp.int32)
    short_table = jnp.stack([kept - start, SLOTS + first, jnp.where(own == hot, taken, 0)])
    long_table = jnp.stack([jnp.zeros_like(bins), SLOTS + bins, jnp.clip(late_count - bins, 0, SPILL)])
    new_amps = place(jnp.where(fits, short_table, long_table), new_rows, backs)
    return (new_amps[None], ladder_share[None])


def solution(mesh):
    return jax.shard_map(
        shards,
        mesh=mesh,
        in_specs=(P("row", "col", None), P("col", None), P(), P(), P("col", None, None), P()),
        out_specs=(P("row", None, "col", None), P("row", "col", None)),
        check_vma=False,
    )
```

```python
import functools

import jax
import jax.numpy as jnp
import numpy as np
from jax import lax
from jax.experimental import pallas as pl
from jax.experimental.pallas import tpu as pltpu
from jax.sharding import PartitionSpec as P

F32 = jnp.float32
BF16 = jnp.bfloat16
BINS = 8
SLOTS = 104
HEAD = 72
TAIL = SLOTS - HEAD
ALL_SLOTS = BINS * SLOTS
SPILL = 18
PAIR_PAD = 896
GROUP_SLOTS = 256
OCC = 40
VMEM_LIMIT = 56 * 1024 * 1024


def split2(x):
    hi = x.astype(BF16)
    return hi, (x - hi.astype(F32)).astype(BF16)


def split3(x):
    hi = x.astype(BF16)
    rest = x - hi.astype(F32)
    mid = rest.astype(BF16)
    return hi, mid, (rest - mid.astype(F32)).astype(BF16)


def dot(a, b):
    return jnp.dot(a, b, preferred_element_type=F32)


def dot_t(a, b):
    return lax.dot_general(a, b, (((1,), (1,)), ((), ())), preferred_element_type=F32)


def iota(shape, dim):
    return lax.broadcasted_iota(jnp.int32, shape, dim)


def prep_kernel(own_ref, group_ref, occ_ref, eocc_ref, w_ref, w_direct, w_mirror, slot_out, group_out, bin_out):
    group = group_ref[...]
    onehot = jnp.where(group == iota((BINS, PAIR_PAD), 0), 1.0, 0.0)
    before = jnp.where(iota((PAIR_PAD, PAIR_PAD), 0) < iota((PAIR_PAD, PAIR_PAD), 1), 1.0, 0.0).astype(BF16)
    rank = jnp.sum(dot(onehot.astype(BF16), before) * onehot, axis=0, keepdims=True)
    valid = jnp.sum(onehot, axis=0, keepdims=True)
    count = jnp.sum(onehot, axis=1, keepdims=True)
    kept = jnp.minimum(count, float(SLOTS))
    spilled = jnp.where(rank >= float(SLOTS), valid, 0.0)
    order = dot(jnp.broadcast_to(spilled, (BINS, PAIR_PAD)).astype(BF16), before)
    total = jnp.sum(spilled, axis=1, keepdims=True)
    free = float(SLOTS) - kept
    short = jnp.minimum(free, float(SPILL))
    fits = jnp.sum(short, axis=0, keepdims=True) >= total
    room = jnp.where(fits, short, free)
    bin_row = iota((BINS, 1), 0)
    first = jnp.zeros((BINS, 1), F32)
    for b in range(BINS - 1):
        first = first + jnp.where(bin_row > b, room[b : b + 1, :], 0.0)
    inside = jnp.where(order >= first, jnp.where(order < first + room, 1.0, 0.0), 0.0)
    is_spilled = spilled > 0.5
    bin_hot = jnp.where(is_spilled, inside, onehot)
    bin_of = jnp.sum(bin_hot * bin_row.astype(F32), axis=0, keepdims=True)
    moved = jnp.sum(inside * (kept - first), axis=0, keepdims=True) + order[0:1, :]
    slot_of = jnp.where(is_spilled, moved, rank)
    in_order = bin_of * float(SLOTS) + slot_of
    tail_first = jnp.where(
        slot_of >= float(HEAD),
        bin_of * float(TAIL) + slot_of - float(HEAD),
        bin_of * float(HEAD) + slot_of + float(BINS * TAIL),
    )
    places = [jnp.where(valid > 0.5, place, -1.0) for place in (in_order, tail_first)]
    own_rank = jnp.where(group == own_ref[0], rank, -1.0)
    stack = jnp.concatenate(places + [own_rank, jnp.zeros((5, PAIR_PAD), F32)], axis=0)
    columns = jnp.transpose(stack, (1, 0)).astype(jnp.int32)
    to_group = jnp.where(columns[:, 2:3] == iota((PAIR_PAD, GROUP_SLOTS), 1), 1.0, 0.0).astype(BF16)
    source = jnp.concatenate([bin_of, slot_of, valid, jnp.zeros((5, PAIR_PAD), F32)], axis=0)
    group_out[...] = dot(source.astype(BF16), to_group).astype(jnp.int32)
    taken = jnp.minimum(jnp.maximum(total - first, 0.0), room)
    bin_cols = jnp.concatenate([count, kept, first, taken, jnp.zeros((BINS, 124), F32)], axis=1)
    bin_out[...] = bin_cols.astype(jnp.int32)

    occ_row = iota((OCC, 1), 0).astype(F32)
    parts = split3(w_ref[...])
    rows = w_ref.shape[0]
    for k, w_out in enumerate((w_direct, w_mirror)):
        to_slot = jnp.where(columns[:, k : k + 1] == iota((PAIR_PAD, ALL_SLOTS), 1), 1.0, 0.0).astype(BF16)
        slots = dot(occ_ref[...].astype(BF16), to_slot)
        slot_i, slot_j, live = slots[0:1, :], slots[1:2, :], slots[2:3, :]
        if k == 0:
            wanted = slot_i * float(OCC) + slot_j
        else:
            wanted = slot_j * float(OCC) + slot_i
            energy = jnp.sum(
                jnp.where(slot_i == occ_row, eocc_ref[...], 0.0), axis=0, keepdims=True
            ) + jnp.sum(jnp.where(slot_j == occ_row, eocc_ref[...], 0.0), axis=0, keepdims=True)
            slot_out[...] = jnp.concatenate([energy, live, jnp.zeros((6, ALL_SLOTS), F32)], axis=0)
        wanted = jnp.where(live > 0.5, wanted, -1.0).astype(jnp.int32)
        w_out[...] = jnp.zeros(w_out.shape, F32)
        for lane in range(0, ALL_SLOTS, 128):
            wide = min(128, ALL_SLOTS - lane)
            pick = jnp.where(
                iota((OCC * OCC, wide), 0) == wanted[:, lane : lane + wide], 1.0, 0.0
            ).astype(BF16)
            w_out[0:rows, lane : lane + wide] = (dot(parts[0], pick) + dot(parts[1], pick)) + dot(
                parts[2], pick
            )


def prep(own, pair_group, e_occ, hole_ladder):
    pairs = pair_group.shape[0]
    first, second = np.triu_indices(OCC)
    occ = np.zeros((8, PAIR_PAD), np.float32)
    occ[0, :pairs], occ[1, :pairs], occ[2, :pairs] = first, second, 1.0
    group = jnp.pad(pair_group, (0, PAIR_PAD - pairs), constant_values=BINS).reshape(1, PAIR_PAD)
    vmem = pl.BlockSpec(memory_space=pltpu.VMEM)
    return pl.pallas_call(
        prep_kernel,
        out_shape=(
            jax.ShapeDtypeStruct((104, ALL_SLOTS), F32),
            jax.ShapeDtypeStruct((104, ALL_SLOTS), F32),
            jax.ShapeDtypeStruct((8, ALL_SLOTS), F32),
            jax.ShapeDtypeStruct((8, GROUP_SLOTS), jnp.int32),
            jax.ShapeDtypeStruct((BINS, 128), jnp.int32),
        ),
        in_specs=[pl.BlockSpec(memory_space=pltpu.SMEM)] + [vmem] * 4,
        out_specs=(vmem,) * 5,
        compiler_params=pltpu.CompilerParams(vmem_limit_bytes=VMEM_LIMIT),
    )(own, group, jnp.asarray(occ), e_occ.reshape(OCC, 1), hole_ladder)


def tile_kernel(t_ref, mirror_hi, mirror_lo, direct_hi, direct_lo):
    for h in range(2):
        for tile in range(5):
            for q in range(8):
                pieces = []
                for e in (2 * q, 2 * q + 1):
                    unit = 5 * tile + e // 3
                    if e < 15 and unit < 24:
                        pieces.append(t_ref[24 * h + unit, 8 * (e % 3) : 8 * (e % 3) + 8, :])
                    else:
                        pieces.append(jnp.zeros((8, 1600), F32))
                hi, lo = split2(jnp.concatenate(pieces, axis=0))
                at = 640 * h + 128 * tile + 16 * q
                mirror_hi[at : at + 16, :] = hi
                mirror_lo[at : at + 16, :] = lo
    for b in range(24):
        hi, lo = split2(t_ref[:, b, :])
        direct_hi[48 * b : 48 * (b + 1), :] = hi
        direct_lo[48 * b : 48 * (b + 1), :] = lo
    direct_hi[1152:1280, :] = jnp.zeros((128, 1600), BF16)
    direct_lo[1152:1280, :] = jnp.zeros((128, 1600), BF16)


def tile_parts(amplitudes):
    vmem = pl.BlockSpec(memory_space=pltpu.VMEM)
    return pl.pallas_call(
        tile_kernel,
        out_shape=(jax.ShapeDtypeStruct((1280, 1600), BF16),) * 4,
        in_specs=[vmem],
        out_specs=(vmem,) * 4,
        compiler_params=pltpu.CompilerParams(vmem_limit_bytes=VMEM_LIMIT),
        cost_estimate=pl.CostEstimate(flops=0, bytes_accessed=60_000_000, transcendentals=0),
    )(amplitudes)


def hole_kernel(mirror, w_ref, t_hi, t_lo, *refs):
    out_refs, (wn, wt_hi, wt_lo) = refs[:-3], refs[-3:]
    for s in range(16):
        wn[100 * s : 100 * s + 100, :] = w_ref[104 * s : 104 * s + 100, :]
    for lane in range(0, ALL_SLOTS, 128):
        wide = min(128, ALL_SLOTS - lane)
        hi, lo = split2(jnp.transpose(wn[:, lane : lane + wide], (1, 0)))
        wt_hi[lane : lane + wide, :] = hi
        wt_lo[lane : lane + wide, :] = lo

    for n in range(5):
        right_hi, right_lo = t_hi[256 * n : 256 * (n + 1), :], t_lo[256 * n : 256 * (n + 1), :]
        y = (dot_t(wt_lo[...], right_hi) + dot_t(wt_hi[...], right_lo)) + dot_t(wt_hi[...], right_hi)
        if mirror:
            for u in range(2):
                h, lane = divmod(2 * n + u, 5)
                first = 0
                for out_ref, size in zip(out_refs, (TAIL, HEAD)):
                    for b in range(BINS):
                        out_ref[b, h, :, 128 * lane : 128 * (lane + 1)] = y[
                            first : first + size, 128 * u : 128 * (u + 1)
                        ]
                        first += size
        else:
            wide = 256 if n < 4 else 128
            for b in range(BINS):
                out_refs[0][b, :, 256 * n : 256 * n + wide] = y[SLOTS * b : SLOTS * (b + 1), 0:wide]


def hole_product(mirror, gathered, hi, lo):
    if mirror:
        shapes = [(BINS, 2, TAIL, 640), (BINS, 2, HEAD, 640)]
    else:
        shapes = [(BINS, SLOTS, 1152)]
    vmem = pl.BlockSpec(memory_space=pltpu.VMEM)
    return pl.pallas_call(
        functools.partial(hole_kernel, mirror),
        out_shape=tuple(jax.ShapeDtypeStruct(shape, F32) for shape in shapes),
        in_specs=[vmem] * 3,
        out_specs=(vmem,) * len(shapes),
        scratch_shapes=[
            pltpu.VMEM((1600, ALL_SLOTS), F32),
            pltpu.VMEM((ALL_SLOTS, 1600), BF16),
            pltpu.VMEM((ALL_SLOTS, 1600), BF16),
        ],
        compiler_params=pltpu.CompilerParams(vmem_limit_bytes=VMEM_LIMIT),
        cost_estimate=pl.CostEstimate(
            flops=2 * 3 * ALL_SLOTS * 1280 * 1600, bytes_accessed=17_000_000, transcendentals=0
        ),
    )(gathered, hi, lo)


def combine_kernel(head, size, *refs):
    if head:
        meta_ref, ed_ref, d_ref, s_ref, eo_ref, ev_ref, ladder_ref, tail_ref, more_ref = refs[:9]
        new_ref, part_ref, m_ref, raw, acc = refs[9:]
    else:
        ed_ref, d_ref, s_ref, eo_ref, ev_ref, ladder_ref = refs[:6]
        raw, part_ref, m_ref, acc = refs[6:]
    step = pl.program_id(0)
    energy = eo_ref[:, 0:1] - ev_ref[...]
    live = eo_ref[:, 1:2] > 0.5
    rows = slice(0, size) if head else slice(SLOTS - size, SLOTS)

    def group(j):
        for u in range(8):
            d = 8 * j + u
            direct = jnp.concatenate([d_ref[r, rows, 48 * u : 48 * (u + 1)] for r in range(8)], axis=1)
            lane = 128 * (d // 5) + 24 * (d % 5)
            mirrored = jnp.concatenate([s_ref[c, :, lane : lane + 24] for c in range(16)], axis=1)
            value = jnp.where(live, (direct + mirrored) / (energy - ed_ref[d]), 0.0)
            m_ref[:, 384 * u : 384 * (u + 1)] = value
            raw[:, u, :] = value

    for j in range(3):
        pl.when(step == j)(functools.partial(group, j))

    if head:
        kept = meta_ref[0]
        new_ref[0:size] = jnp.where(iota((size, 8, 384), 0) < kept, raw[...], 0.0)
        tail = iota((SLOTS - size, 8, 384), 0) + size
        new_ref[size:SLOTS] = jnp.where(tail < kept, tail_ref[...], 0.0)
        new_ref[SLOTS:] = jnp.zeros((new_ref.shape[0] - SLOTS, 8, 384), F32)

    left_hi, left_lo = split2(m_ref[...])
    right_hi, right_lo = split2(ladder_ref[...].reshape(8 * 384, 256))
    term = (dot(left_lo, right_hi) + dot(left_hi, right_lo)) + dot(left_hi, right_hi)

    @pl.when(step == 0)
    def _():
        acc[...] = jnp.zeros(acc.shape, F32)
        if head:
            acc[size:SLOTS, :] = more_ref[...]

    acc[0:size, :] += term

    @pl.when(step == 2)
    def _():
        part_ref[...] = jnp.transpose(acc[...], (1, 0)) if head else acc[...]


def combine(size, ed, direct, mirrored, energy, ev, ladder, head=None, rows=0):
    smem = pl.BlockSpec(memory_space=pltpu.SMEM)
    in_specs = [
        smem,
        pl.BlockSpec((8, SLOTS, 384), lambda j: (0, 0, j)),
        pl.BlockSpec((16, size, 640), lambda j: (0, 0, 0)),
        pl.BlockSpec((size, 2), lambda j: (0, 0)),
        pl.BlockSpec((1, 384), lambda j: (0, 0)),
        pl.BlockSpec((8, 384, 256), lambda j: (j, 0, 0)),
    ]
    operands = [ed, direct, mirrored, energy, ev, ladder]
    scratch = [pltpu.VMEM((size, 8 * 384), F32)]
    if head is None:
        out_shape = (jax.ShapeDtypeStruct((size, 24, 384), F32), jax.ShapeDtypeStruct((size, 256), F32))
        out_specs = (
            pl.BlockSpec((size, 8, 384), lambda j: (0, j, 0)),
            pl.BlockSpec((size, 256), lambda j: (0, 0)),
        )
        scratch += [pltpu.VMEM((size, 256), F32)]
    else:
        meta, tail, more = head
        operands = [meta] + operands + [tail, more]
        in_specs = [smem] + in_specs + [
            pl.BlockSpec((SLOTS - size, 8, 384), lambda j: (0, j, 0)),
            pl.BlockSpec((SLOTS - size, 256), lambda j: (0, 0)),
        ]
        out_shape = (jax.ShapeDtypeStruct((rows, 24, 384), F32), jax.ShapeDtypeStruct((256, 128), F32))
        out_specs = (
            pl.BlockSpec((rows, 8, 384), lambda j: (0, j, 0)),
            pl.BlockSpec((256, 128), lambda j: (0, 0)),
        )
        scratch += [pltpu.VMEM((size, 8, 384), F32), pltpu.VMEM((128, 256), F32)]
    return pl.pallas_call(
        functools.partial(combine_kernel, head is not None, size),
        grid=(3,),
        out_shape=out_shape,
        in_specs=in_specs,
        out_specs=out_specs,
        scratch_shapes=scratch,
        compiler_params=pltpu.CompilerParams(vmem_limit_bytes=VMEM_LIMIT),
        cost_estimate=pl.CostEstimate(
            flops=2 * 3 * 128 * 9216 * 256, bytes_accessed=40_000_000, transcendentals=0
        ),
    )(*operands)


def place_kernel(table_ref, new_ref, back_ref, out_ref, sem):
    rows = table_ref[2, 0]

    def send(k, carry):
        pltpu.make_async_copy(back_ref.at[table_ref[0, k]], out_ref.at[SLOTS + k], sem).start()
        return carry

    lax.fori_loop(0, rows, send, 0)

    def wait(k, carry):
        pltpu.make_async_copy(back_ref.at[0], out_ref.at[SLOTS], sem).wait()
        return carry

    lax.fori_loop(0, rows, wait, 0)


def place(table, new, back):
    hbm = pl.BlockSpec(memory_space=pl.ANY)
    vmem = pl.BlockSpec(memory_space=pltpu.VMEM)
    return pl.pallas_call(
        place_kernel,
        out_shape=jax.ShapeDtypeStruct(new.shape, F32),
        in_specs=[pl.BlockSpec(memory_space=pltpu.SMEM), hbm, vmem],
        out_specs=hbm,
        scratch_shapes=[pltpu.SemaphoreType.DMA],
        input_output_aliases={1: 0},
        compiler_params=pltpu.CompilerParams(vmem_limit_bytes=VMEM_LIMIT),
    )(table, new, back)


def nothing_kernel(x_ref, other_ref, out_ref):
    del x_ref, other_ref, out_ref


def after(x, other):
    hbm = pl.BlockSpec(memory_space=pl.ANY)
    return pl.pallas_call(
        nothing_kernel,
        out_shape=jax.ShapeDtypeStruct(x.shape, x.dtype),
        in_specs=[hbm, hbm],
        out_specs=hbm,
        input_output_aliases={0: 0},
    )(x, other)


def shards(amplitudes, hole_ladder, e_occ, e_vir, ladder_ints, pair_group):
    tile_cols = amplitudes.shape[1]
    capacity = 2 * pair_group.shape[0] // lax.axis_size("row")
    own = lax.axis_index("row")
    col_index = lax.axis_index("col")

    w_direct, w_mirror, slot_table, group_table, bin_table = prep(
        own.reshape(1), pair_group, e_occ, hole_ladder
    )
    w_direct = lax.all_gather(w_direct, "col", axis=0, tiled=True)
    w_mirror = lax.all_gather(w_mirror, "col", axis=0, tiled=True)
    mirror_hi, mirror_lo, direct_hi, direct_lo = tile_parts(amplitudes)

    direct = hole_product(False, w_direct, direct_hi, direct_lo)[0]
    direct = lax.all_to_all(direct, "row", 0, 0)
    tail_part, head_part = hole_product(True, w_mirror, mirror_hi, mirror_lo)

    def mirror_exchange(part, size):
        part = lax.all_to_all(part, "row", 0, 0).reshape(16, size, 640)
        return lax.all_to_all(part, "col", 0, 0)

    tail_mirror = mirror_exchange(after(tail_part, direct), TAIL)

    def own_slots(first, size):
        return lax.dynamic_slice(slot_table, (0, first + own * size), (2, size)).T

    tail_energy, head_energy = own_slots(0, TAIL), own_slots(BINS * TAIL, HEAD)
    local_energy = lax.dynamic_slice_in_dim(e_vir, col_index * tile_cols, tile_cols)
    virtual = e_vir.reshape(1, -1)
    counts, kept, taken = bin_table[:, 0], bin_table[:, 1], bin_table[:, 3]
    own_count = lax.dynamic_index_in_dim(counts, own, 0, False)
    own_kept = jnp.minimum(own_count, SLOTS)
    start = jnp.minimum(kept, SLOTS - SPILL)
    own_start = lax.dynamic_index_in_dim(start, own, 0, False)
    fits = (jnp.max(taken) <= SPILL) & jnp.all((taken == 0) | (kept >= HEAD))

    late_rows, late_part = combine(
        TAIL, local_energy, direct, tail_mirror, tail_energy, virtual, ladder_ints
    )
    head_mirror = mirror_exchange(after(head_part, late_part), HEAD)
    segment = lax.dynamic_slice_in_dim(late_rows, jnp.maximum(own_start - HEAD, 0), SPILL, 0)
    back = lax.all_gather(segment, "row", axis=0, tiled=True)

    def whole(meta, direct, head_mirror, late_rows):
        return combine(
            HEAD, local_energy, direct, head_mirror, head_energy, virtual, ladder_ints,
            (meta, late_rows, late_part), capacity,
        )

    new_rows, partial_value = whole(own_kept.reshape(1), direct, head_mirror, late_rows)

    blocks = lax.all_to_all(partial_value.reshape(16, 16, 128), "col", 0, 0)
    share = jnp.sum(blocks, axis=0)
    shares = lax.all_to_all(jnp.broadcast_to(share, (BINS, 16, 128)), "row", 0, 0)
    live = group_table[2, :capacity]
    from_bin, from_slot = group_table[0, :capacity], group_table[1, :capacity]
    where_from = jnp.where(live > 0, from_bin * 128 + from_slot, -1)
    pick = jnp.arange(BINS * 128, dtype=jnp.int32)[:, None] == where_from[None, :]
    ladder_share = jnp.dot(
        jnp.transpose(shares, (1, 0, 2)).reshape(16, BINS * 128),
        pick.astype(F32),
        precision=lax.Precision.HIGHEST,
        preferred_element_type=F32,
    )

    late_bin, late_slot = from_bin[SLOTS:], from_slot[SLOTS:]
    late_count = own_count - own_kept
    bin_start = jnp.sum(jnp.where(late_bin[:, None] == jnp.arange(BINS)[None, :], start[None, :], 0), axis=1)
    back_row = jnp.clip(late_bin * SPILL + late_slot - bin_start, 0, BINS * SPILL - 1)
    count_row = jnp.full_like(back_row, jnp.where(fits, late_count, 0))
    new_amps = place(jnp.stack([back_row, back_row, count_row]), new_rows, back)

    def long_way(carry):
        turn, new_amps, direct, head_mirror, late_rows = carry
        values, _ = whole(jnp.full((1,), SLOTS, jnp.int32) + turn, direct, head_mirror, late_rows)
        everything = lax.all_gather(values[:SLOTS], "row", axis=0, tiled=True)
        late = everything[late_bin * SLOTS + late_slot]
        rows = jnp.arange(capacity - SLOTS, dtype=jnp.int32)
        table = jnp.stack([rows, rows, jnp.full_like(rows, late_count)])
        return turn + 1, place(table, new_amps, late), direct, head_mirror, late_rows

    turns = jnp.where(fits, 0, 1)
    new_amps = lax.while_loop(
        lambda carry: carry[0] < turns, long_way, (jnp.int32(0), new_amps, direct, head_mirror, late_rows)
    )[1]
    return (new_amps[None], ladder_share[None])


def solution(mesh):
    return jax.shard_map(
        shards,
        mesh=mesh,
        in_specs=(P("row", "col", None), P("col", None), P(), P(), P("col", None, None), P()),
        out_specs=(P("row", None, "col", None), P("row", "col", None)),
        check_vma=False,
    )
```

```python
import functools

import jax
import jax.numpy as jnp
import numpy as np
from jax import lax
from jax.experimental import pallas as pl
from jax.experimental.pallas import tpu as pltpu
from jax.sharding import PartitionSpec as P

F32 = jnp.float32
BF16 = jnp.bfloat16
BINS = 8
SLOTS = 104
HEAD = 72
TAIL = SLOTS - HEAD
ALL_SLOTS = BINS * SLOTS
SPILL = 18
PAIR_PAD = 896
GROUP_SLOTS = 256
OCC = 40
VMEM_LIMIT = 56 * 1024 * 1024


def split2(x):
    hi = x.astype(BF16)
    return hi, (x - hi.astype(F32)).astype(BF16)


def split3(x):
    hi = x.astype(BF16)
    rest = x - hi.astype(F32)
    mid = rest.astype(BF16)
    return hi, mid, (rest - mid.astype(F32)).astype(BF16)


def dot(a, b):
    return jnp.dot(a, b, preferred_element_type=F32)


def dot_t(a, b):
    return lax.dot_general(a, b, (((1,), (1,)), ((), ())), preferred_element_type=F32)


def iota(shape, dim):
    return lax.broadcasted_iota(jnp.int32, shape, dim)


def prep_kernel(own_ref, group_ref, occ_ref, eocc_ref, w_ref, w_direct, w_mirror, slot_out, group_out, bin_out):
    group = group_ref[...]
    onehot = jnp.where(group == iota((BINS, PAIR_PAD), 0), 1.0, 0.0)
    before = jnp.where(iota((PAIR_PAD, PAIR_PAD), 0) < iota((PAIR_PAD, PAIR_PAD), 1), 1.0, 0.0).astype(BF16)
    rank = jnp.sum(dot(onehot.astype(BF16), before) * onehot, axis=0, keepdims=True)
    valid = jnp.sum(onehot, axis=0, keepdims=True)
    count = jnp.sum(onehot, axis=1, keepdims=True)
    kept = jnp.minimum(count, float(SLOTS))
    spilled = jnp.where(rank >= float(SLOTS), valid, 0.0)
    order = dot(jnp.broadcast_to(spilled, (BINS, PAIR_PAD)).astype(BF16), before)
    total = jnp.sum(spilled, axis=1, keepdims=True)
    free = float(SLOTS) - kept
    short = jnp.minimum(free, float(SPILL))
    fits = jnp.sum(short, axis=0, keepdims=True) >= total
    room = jnp.where(fits, short, free)
    bin_row = iota((BINS, 1), 0)
    first = jnp.zeros((BINS, 1), F32)
    for b in range(BINS - 1):
        first = first + jnp.where(bin_row > b, room[b : b + 1, :], 0.0)
    inside = jnp.where(order >= first, jnp.where(order < first + room, 1.0, 0.0), 0.0)
    is_spilled = spilled > 0.5
    bin_hot = jnp.where(is_spilled, inside, onehot)
    bin_of = jnp.sum(bin_hot * bin_row.astype(F32), axis=0, keepdims=True)
    moved = jnp.sum(inside * (kept - first), axis=0, keepdims=True) + order[0:1, :]
    slot_of = jnp.where(is_spilled, moved, rank)
    in_order = bin_of * float(SLOTS) + slot_of
    tail_first = jnp.where(
        slot_of >= float(HEAD),
        bin_of * float(TAIL) + slot_of - float(HEAD),
        bin_of * float(HEAD) + slot_of + float(BINS * TAIL),
    )
    places = [jnp.where(valid > 0.5, place, -1.0) for place in (in_order, tail_first)]
    own_rank = jnp.where(group == own_ref[0], rank, -1.0)
    stack = jnp.concatenate(places + [own_rank, jnp.zeros((5, PAIR_PAD), F32)], axis=0)
    columns = jnp.transpose(stack, (1, 0)).astype(jnp.int32)
    to_group = jnp.where(columns[:, 2:3] == iota((PAIR_PAD, GROUP_SLOTS), 1), 1.0, 0.0).astype(BF16)
    source = jnp.concatenate([bin_of, slot_of, valid, jnp.zeros((5, PAIR_PAD), F32)], axis=0)
    group_out[...] = dot(source.astype(BF16), to_group).astype(jnp.int32)
    taken = jnp.minimum(jnp.maximum(total - first, 0.0), room)
    bin_cols = jnp.concatenate([count, kept, first, taken, jnp.zeros((BINS, 124), F32)], axis=1)
    bin_out[...] = bin_cols.astype(jnp.int32)

    occ_row = iota((OCC, 1), 0).astype(F32)
    parts = split3(w_ref[...])
    rows = w_ref.shape[0]
    for k, w_out in enumerate((w_direct, w_mirror)):
        to_slot = jnp.where(columns[:, k : k + 1] == iota((PAIR_PAD, ALL_SLOTS), 1), 1.0, 0.0).astype(BF16)
        slots = dot(occ_ref[...].astype(BF16), to_slot)
        slot_i, slot_j, live = slots[0:1, :], slots[1:2, :], slots[2:3, :]
        if k == 0:
            wanted = slot_i * float(OCC) + slot_j
        else:
            wanted = slot_j * float(OCC) + slot_i
            energy = jnp.sum(
                jnp.where(slot_i == occ_row, eocc_ref[...], 0.0), axis=0, keepdims=True
            ) + jnp.sum(jnp.where(slot_j == occ_row, eocc_ref[...], 0.0), axis=0, keepdims=True)
            slot_out[...] = jnp.concatenate([energy, live, jnp.zeros((6, ALL_SLOTS), F32)], axis=0)
        wanted = jnp.where(live > 0.5, wanted, -1.0).astype(jnp.int32)
        w_out[...] = jnp.zeros(w_out.shape, F32)
        for lane in range(0, ALL_SLOTS, 128):
            wide = min(128, ALL_SLOTS - lane)
            pick = jnp.where(
                iota((OCC * OCC, wide), 0) == wanted[:, lane : lane + wide], 1.0, 0.0
            ).astype(BF16)
            w_out[0:rows, lane : lane + wide] = (dot(parts[0], pick) + dot(parts[1], pick)) + dot(
                parts[2], pick
            )


def prep(own, pair_group, e_occ, hole_ladder):
    pairs = pair_group.shape[0]
    first, second = np.triu_indices(OCC)
    occ = np.zeros((8, PAIR_PAD), np.float32)
    occ[0, :pairs], occ[1, :pairs], occ[2, :pairs] = first, second, 1.0
    group = jnp.pad(pair_group, (0, PAIR_PAD - pairs), constant_values=BINS).reshape(1, PAIR_PAD)
    vmem = pl.BlockSpec(memory_space=pltpu.VMEM)
    return pl.pallas_call(
        prep_kernel,
        out_shape=(
            jax.ShapeDtypeStruct((104, ALL_SLOTS), F32),
            jax.ShapeDtypeStruct((104, ALL_SLOTS), F32),
            jax.ShapeDtypeStruct((8, ALL_SLOTS), F32),
            jax.ShapeDtypeStruct((8, GROUP_SLOTS), jnp.int32),
            jax.ShapeDtypeStruct((BINS, 128), jnp.int32),
        ),
        in_specs=[pl.BlockSpec(memory_space=pltpu.SMEM)] + [vmem] * 4,
        out_specs=(vmem,) * 5,
        compiler_params=pltpu.CompilerParams(vmem_limit_bytes=VMEM_LIMIT),
    )(own, group, jnp.asarray(occ), e_occ.reshape(OCC, 1), hole_ladder)


def tile_kernel(t_ref, mirror_hi, mirror_lo, direct_hi, direct_lo):
    for h in range(2):
        for tile in range(5):
            for q in range(8):
                pieces = []
                for e in (2 * q, 2 * q + 1):
                    unit = 5 * tile + e // 3
                    if e < 15 and unit < 24:
                        pieces.append(t_ref[24 * h + unit, 8 * (e % 3) : 8 * (e % 3) + 8, :])
                    else:
                        pieces.append(jnp.zeros((8, 1600), F32))
                hi, lo = split2(jnp.concatenate(pieces, axis=0))
                at = 640 * h + 128 * tile + 16 * q
                mirror_hi[at : at + 16, :] = hi
                mirror_lo[at : at + 16, :] = lo
    for b in range(24):
        hi, lo = split2(t_ref[:, b, :])
        direct_hi[48 * b : 48 * (b + 1), :] = hi
        direct_lo[48 * b : 48 * (b + 1), :] = lo
    direct_hi[1152:1280, :] = jnp.zeros((128, 1600), BF16)
    direct_lo[1152:1280, :] = jnp.zeros((128, 1600), BF16)


def tile_parts(amplitudes):
    vmem = pl.BlockSpec(memory_space=pltpu.VMEM)
    return pl.pallas_call(
        tile_kernel,
        out_shape=(jax.ShapeDtypeStruct((1280, 1600), BF16),) * 4,
        in_specs=[vmem],
        out_specs=(vmem,) * 4,
        compiler_params=pltpu.CompilerParams(vmem_limit_bytes=VMEM_LIMIT),
        cost_estimate=pl.CostEstimate(flops=0, bytes_accessed=60_000_000, transcendentals=0),
    )(amplitudes)


def hole_kernel(mirror, w_ref, t_hi, t_lo, out_ref, wn, wt_hi, wt_lo):
    for s in range(16):
        wn[100 * s : 100 * s + 100, :] = w_ref[104 * s : 104 * s + 100, :]
    for lane in range(0, ALL_SLOTS, 128):
        wide = min(128, ALL_SLOTS - lane)
        hi, lo = split2(jnp.transpose(wn[:, lane : lane + wide], (1, 0)))
        wt_hi[lane : lane + wide, :] = hi
        wt_lo[lane : lane + wide, :] = lo

    for n in range(5):
        right_hi, right_lo = t_hi[256 * n : 256 * (n + 1), :], t_lo[256 * n : 256 * (n + 1), :]
        y = (dot_t(wt_lo[...], right_hi) + dot_t(wt_hi[...], right_lo)) + dot_t(wt_hi[...], right_hi)
        if mirror:
            for u in range(2):
                h, lane = divmod(2 * n + u, 5)
                first = 0
                for slots in (slice(HEAD, SLOTS), slice(0, HEAD)):
                    for b in range(BINS):
                        last = first + slots.stop - slots.start
                        out_ref[b, h, slots, 128 * lane : 128 * (lane + 1)] = y[
                            first:last, 128 * u : 128 * (u + 1)
                        ]
                        first = last
        else:
            wide = 256 if n < 4 else 128
            for b in range(BINS):
                out_ref[b, :, 256 * n : 256 * n + wide] = y[SLOTS * b : SLOTS * (b + 1), 0:wide]


def hole_product(mirror, gathered, hi, lo):
    shape = (BINS, 2, SLOTS, 640) if mirror else (BINS, SLOTS, 1152)
    vmem = pl.BlockSpec(memory_space=pltpu.VMEM)
    return pl.pallas_call(
        functools.partial(hole_kernel, mirror),
        out_shape=jax.ShapeDtypeStruct(shape, F32),
        in_specs=[vmem] * 3,
        out_specs=vmem,
        scratch_shapes=[
            pltpu.VMEM((1600, ALL_SLOTS), F32),
            pltpu.VMEM((ALL_SLOTS, 1600), BF16),
            pltpu.VMEM((ALL_SLOTS, 1600), BF16),
        ],
        compiler_params=pltpu.CompilerParams(vmem_limit_bytes=VMEM_LIMIT),
        cost_estimate=pl.CostEstimate(
            flops=2 * 3 * ALL_SLOTS * 1280 * 1600, bytes_accessed=17_000_000, transcendentals=0
        ),
    )(gathered, hi, lo)


def combine_kernel(head, size, *refs):
    if head:
        meta_ref, ed_ref, d_ref, s_ref, eo_ref, ev_ref, ladder_ref, tail_ref, more_ref = refs[:9]
        new_ref, part_ref, m_ref, raw, acc = refs[9:]
    else:
        ed_ref, d_ref, s_ref, eo_ref, ev_ref, ladder_ref = refs[:6]
        raw, part_ref, m_ref, acc = refs[6:]
    step = pl.program_id(0)
    energy = eo_ref[:, 0:1] - ev_ref[...]
    live = eo_ref[:, 1:2] > 0.5
    rows = slice(0, size) if head else slice(SLOTS - size, SLOTS)

    def group(j):
        for u in range(8):
            d = 8 * j + u
            direct = jnp.concatenate([d_ref[r, rows, 48 * u : 48 * (u + 1)] for r in range(8)], axis=1)
            lane = 128 * (d // 5) + 24 * (d % 5)
            mirrored = jnp.concatenate([s_ref[c, :, lane : lane + 24] for c in range(16)], axis=1)
            value = jnp.where(live, (direct + mirrored) / (energy - ed_ref[d]), 0.0)
            m_ref[:, 384 * u : 384 * (u + 1)] = value
            raw[:, u, :] = value

    for j in range(3):
        pl.when(step == j)(functools.partial(group, j))

    if head:
        kept = meta_ref[0]
        new_ref[0:size] = jnp.where(iota((size, 8, 384), 0) < kept, raw[...], 0.0)
        tail = iota((SLOTS - size, 8, 384), 0) + size
        new_ref[size:SLOTS] = jnp.where(tail < kept, tail_ref[...], 0.0)
        new_ref[SLOTS:] = jnp.zeros((new_ref.shape[0] - SLOTS, 8, 384), F32)

    left_hi, left_lo = split2(m_ref[...])
    right_hi, right_lo = split2(ladder_ref[...].reshape(8 * 384, 256))
    term = (dot(left_lo, right_hi) + dot(left_hi, right_lo)) + dot(left_hi, right_hi)

    @pl.when(step == 0)
    def _():
        acc[...] = jnp.zeros(acc.shape, F32)
        if head:
            acc[size:SLOTS, :] = more_ref[...]

    acc[0:size, :] += term

    @pl.when(step == 2)
    def _():
        part_ref[...] = jnp.transpose(acc[...], (1, 0)) if head else acc[...]


def combine(size, ed, direct, mirrored, energy, ev, ladder, head=None, rows=0):
    smem = pl.BlockSpec(memory_space=pltpu.SMEM)
    in_specs = [
        smem,
        pl.BlockSpec((8, SLOTS, 384), lambda j: (0, 0, j)),
        pl.BlockSpec((16, size, 640), lambda j: (0, 0, 0)),
        pl.BlockSpec((size, 2), lambda j: (0, 0)),
        pl.BlockSpec((1, 384), lambda j: (0, 0)),
        pl.BlockSpec((8, 384, 256), lambda j: (j, 0, 0)),
    ]
    operands = [ed, direct, mirrored, energy, ev, ladder]
    scratch = [pltpu.VMEM((size, 8 * 384), F32)]
    if head is None:
        out_shape = (jax.ShapeDtypeStruct((size, 24, 384), F32), jax.ShapeDtypeStruct((size, 256), F32))
        out_specs = (
            pl.BlockSpec((size, 8, 384), lambda j: (0, j, 0)),
            pl.BlockSpec((size, 256), lambda j: (0, 0)),
        )
        scratch += [pltpu.VMEM((size, 256), F32)]
    else:
        meta, tail, more = head
        operands = [meta] + operands + [tail, more]
        in_specs = [smem] + in_specs + [
            pl.BlockSpec((SLOTS - size, 8, 384), lambda j: (0, j, 0)),
            pl.BlockSpec((SLOTS - size, 256), lambda j: (0, 0)),
        ]
        out_shape = (jax.ShapeDtypeStruct((rows, 24, 384), F32), jax.ShapeDtypeStruct((256, 128), F32))
        out_specs = (
            pl.BlockSpec((rows, 8, 384), lambda j: (0, j, 0)),
            pl.BlockSpec((256, 128), lambda j: (0, 0)),
        )
        scratch += [pltpu.VMEM((size, 8, 384), F32), pltpu.VMEM((128, 256), F32)]
    return pl.pallas_call(
        functools.partial(combine_kernel, head is not None, size),
        grid=(3,),
        out_shape=out_shape,
        in_specs=in_specs,
        out_specs=out_specs,
        scratch_shapes=scratch,
        compiler_params=pltpu.CompilerParams(vmem_limit_bytes=VMEM_LIMIT),
        cost_estimate=pl.CostEstimate(
            flops=2 * 3 * 128 * 9216 * 256, bytes_accessed=40_000_000, transcendentals=0
        ),
    )(*operands)


def place_kernel(table_ref, new_ref, back_ref, out_ref, sem):
    rows = table_ref[2, 0]

    def send(k, carry):
        pltpu.make_async_copy(back_ref.at[table_ref[0, k]], out_ref.at[SLOTS + k], sem).start()
        return carry

    lax.fori_loop(0, rows, send, 0)

    def wait(k, carry):
        pltpu.make_async_copy(back_ref.at[0], out_ref.at[SLOTS], sem).wait()
        return carry

    lax.fori_loop(0, rows, wait, 0)


def place(table, new, back):
    hbm = pl.BlockSpec(memory_space=pl.ANY)
    vmem = pl.BlockSpec(memory_space=pltpu.VMEM)
    return pl.pallas_call(
        place_kernel,
        out_shape=jax.ShapeDtypeStruct(new.shape, F32),
        in_specs=[pl.BlockSpec(memory_space=pltpu.SMEM), hbm, vmem],
        out_specs=hbm,
        scratch_shapes=[pltpu.SemaphoreType.DMA],
        input_output_aliases={1: 0},
        compiler_params=pltpu.CompilerParams(vmem_limit_bytes=VMEM_LIMIT),
    )(table, new, back)


def nothing_kernel(x_ref, other_ref, out_ref):
    del x_ref, other_ref, out_ref


def after(x, other):
    hbm = pl.BlockSpec(memory_space=pl.ANY)
    return pl.pallas_call(
        nothing_kernel,
        out_shape=jax.ShapeDtypeStruct(x.shape, x.dtype),
        in_specs=[hbm, hbm],
        out_specs=hbm,
        input_output_aliases={0: 0},
    )(x, other)


def shards(amplitudes, hole_ladder, e_occ, e_vir, ladder_ints, pair_group):
    tile_cols = amplitudes.shape[1]
    capacity = 2 * pair_group.shape[0] // lax.axis_size("row")
    own = lax.axis_index("row")
    col_index = lax.axis_index("col")

    w_direct, w_mirror, slot_table, group_table, bin_table = prep(
        own.reshape(1), pair_group, e_occ, hole_ladder
    )
    w_direct = lax.all_gather(w_direct, "col", axis=0, tiled=True)
    w_mirror = lax.all_gather(w_mirror, "col", axis=0, tiled=True)
    mirror_hi, mirror_lo, direct_hi, direct_lo = tile_parts(amplitudes)

    direct = hole_product(False, w_direct, direct_hi, direct_lo)
    direct = lax.all_to_all(direct, "row", 0, 0)
    mirror = after(hole_product(True, w_mirror, mirror_hi, mirror_lo), direct)
    mirror = lax.all_to_all(mirror, "row", 0, 0).reshape(16, SLOTS, 640)
    tail_mirror = lax.all_to_all(mirror[:, HEAD:], "col", 0, 0)
    head_mirror = lax.all_to_all(after(mirror[:, :HEAD], tail_mirror), "col", 0, 0)

    def own_slots(first, size):
        return lax.dynamic_slice(slot_table, (0, first + own * size), (2, size)).T

    tail_energy, head_energy = own_slots(0, TAIL), own_slots(BINS * TAIL, HEAD)
    local_energy = lax.dynamic_slice_in_dim(e_vir, col_index * tile_cols, tile_cols)
    virtual = e_vir.reshape(1, -1)
    counts, kept, taken = bin_table[:, 0], bin_table[:, 1], bin_table[:, 3]
    own_count = lax.dynamic_index_in_dim(counts, own, 0, False)
    own_kept = jnp.minimum(own_count, SLOTS)
    start = jnp.minimum(kept, SLOTS - SPILL)
    own_start = lax.dynamic_index_in_dim(start, own, 0, False)
    fits = (jnp.max(taken) <= SPILL) & jnp.all((taken == 0) | (kept >= HEAD))

    late_rows, late_part = combine(
        TAIL, local_energy, direct, tail_mirror, tail_energy, virtual, ladder_ints
    )
    segment = lax.dynamic_slice_in_dim(late_rows, jnp.maximum(own_start - HEAD, 0), SPILL, 0)
    back = lax.all_gather(segment, "row", axis=0, tiled=True)

    def whole(meta, direct, head_mirror, late_rows):
        return combine(
            HEAD, local_energy, direct, head_mirror, head_energy, virtual, ladder_ints,
            (meta, late_rows, late_part), capacity,
        )

    new_rows, partial_value = whole(own_kept.reshape(1), direct, head_mirror, late_rows)

    blocks = lax.all_to_all(partial_value.reshape(16, 16, 128), "col", 0, 0)
    share = jnp.sum(blocks, axis=0)
    shares = lax.all_to_all(jnp.broadcast_to(share, (BINS, 16, 128)), "row", 0, 0)
    live = group_table[2, :capacity]
    from_bin, from_slot = group_table[0, :capacity], group_table[1, :capacity]
    where_from = jnp.where(live > 0, from_bin * 128 + from_slot, -1)
    pick = jnp.arange(BINS * 128, dtype=jnp.int32)[:, None] == where_from[None, :]
    ladder_share = jnp.dot(
        jnp.transpose(shares, (1, 0, 2)).reshape(16, BINS * 128),
        pick.astype(F32),
        precision=lax.Precision.HIGHEST,
        preferred_element_type=F32,
    )

    late_bin, late_slot = from_bin[SLOTS:], from_slot[SLOTS:]
    late_count = own_count - own_kept
    bin_start = jnp.sum(jnp.where(late_bin[:, None] == jnp.arange(BINS)[None, :], start[None, :], 0), axis=1)
    back_row = jnp.clip(late_bin * SPILL + late_slot - bin_start, 0, BINS * SPILL - 1)
    count_row = jnp.full_like(back_row, jnp.where(fits, late_count, 0))
    new_amps = place(jnp.stack([back_row, back_row, count_row]), new_rows, back)

    def long_way(carry):
        turn, new_amps, direct, head_mirror, late_rows = carry
        values, _ = whole(jnp.full((1,), SLOTS, jnp.int32) + turn, direct, head_mirror, late_rows)
        everything = lax.all_gather(values[:SLOTS], "row", axis=0, tiled=True)
        late = everything[late_bin * SLOTS + late_slot]
        rows = jnp.arange(capacity - SLOTS, dtype=jnp.int32)
        table = jnp.stack([rows, rows, jnp.full_like(rows, late_count)])
        return turn + 1, place(table, new_amps, late), direct, head_mirror, late_rows

    turns = jnp.where(fits, 0, 1)
    new_amps = lax.while_loop(
        lambda carry: carry[0] < turns, long_way, (jnp.int32(0), new_amps, direct, head_mirror, late_rows)
    )[1]
    return (new_amps[None], ladder_share[None])


def solution(mesh):
    return jax.shard_map(
        shards,
        mesh=mesh,
        in_specs=(P("row", "col", None), P("col", None), P(), P(), P("col", None, None), P()),
        out_specs=(P("row", None, "col", None), P("row", "col", None)),
        check_vma=False,
    )
```

```python
import functools

import jax
import jax.numpy as jnp
import numpy as np
from jax import lax
from jax.experimental import pallas as pl
from jax.experimental.pallas import tpu as pltpu
from jax.sharding import PartitionSpec as P

F32 = jnp.float32
BF16 = jnp.bfloat16
BINS = 8
SLOTS = 104
HEAD = 72
TAIL = SLOTS - HEAD
ALL_SLOTS = BINS * SLOTS
SPILL = 18
PAIR_PAD = 896
GROUP_SLOTS = 256
OCC = 40
VMEM_LIMIT = 56 * 1024 * 1024


def split2(x):
    hi = x.astype(BF16)
    return hi, (x - hi.astype(F32)).astype(BF16)


def split3(x):
    hi = x.astype(BF16)
    rest = x - hi.astype(F32)
    mid = rest.astype(BF16)
    return hi, mid, (rest - mid.astype(F32)).astype(BF16)


def dot(a, b):
    return jnp.dot(a, b, preferred_element_type=F32)


def dot_t(a, b):
    return lax.dot_general(a, b, (((1,), (1,)), ((), ())), preferred_element_type=F32)


def iota(shape, dim):
    return lax.broadcasted_iota(jnp.int32, shape, dim)


def prep_kernel(own_ref, group_ref, occ_ref, eocc_ref, w_ref, w_direct, w_mirror, slot_out, group_out, bin_out):
    group = group_ref[...]
    onehot = jnp.where(group == iota((BINS, PAIR_PAD), 0), 1.0, 0.0)
    before = jnp.where(iota((PAIR_PAD, PAIR_PAD), 0) < iota((PAIR_PAD, PAIR_PAD), 1), 1.0, 0.0).astype(BF16)
    rank = jnp.sum(dot(onehot.astype(BF16), before) * onehot, axis=0, keepdims=True)
    valid = jnp.sum(onehot, axis=0, keepdims=True)
    count = jnp.sum(onehot, axis=1, keepdims=True)
    kept = jnp.minimum(count, float(SLOTS))
    spilled = jnp.where(rank >= float(SLOTS), valid, 0.0)
    order = dot(jnp.broadcast_to(spilled, (BINS, PAIR_PAD)).astype(BF16), before)
    total = jnp.sum(spilled, axis=1, keepdims=True)
    free = float(SLOTS) - kept
    short = jnp.minimum(free, float(SPILL))
    fits = jnp.sum(short, axis=0, keepdims=True) >= total
    room = jnp.where(fits, short, free)
    bin_row = iota((BINS, 1), 0)
    first = jnp.zeros((BINS, 1), F32)
    for b in range(BINS - 1):
        first = first + jnp.where(bin_row > b, room[b : b + 1, :], 0.0)
    inside = jnp.where(order >= first, jnp.where(order < first + room, 1.0, 0.0), 0.0)
    is_spilled = spilled > 0.5
    bin_hot = jnp.where(is_spilled, inside, onehot)
    bin_of = jnp.sum(bin_hot * bin_row.astype(F32), axis=0, keepdims=True)
    moved = jnp.sum(inside * (kept - first), axis=0, keepdims=True) + order[0:1, :]
    slot_of = jnp.where(is_spilled, moved, rank)
    in_bin = bin_of * float(SLOTS) + jnp.where(
        slot_of >= float(HEAD), slot_of - float(HEAD), slot_of + float(TAIL)
    )
    tail_first = jnp.where(
        slot_of >= float(HEAD),
        bin_of * float(TAIL) + slot_of - float(HEAD),
        bin_of * float(HEAD) + slot_of + float(BINS * TAIL),
    )
    places = [jnp.where(valid > 0.5, place, -1.0) for place in (in_bin, tail_first)]
    own_rank = jnp.where(group == own_ref[0], rank, -1.0)
    stack = jnp.concatenate(places + [own_rank, jnp.zeros((5, PAIR_PAD), F32)], axis=0)
    columns = jnp.transpose(stack, (1, 0)).astype(jnp.int32)
    to_group = jnp.where(columns[:, 2:3] == iota((PAIR_PAD, GROUP_SLOTS), 1), 1.0, 0.0).astype(BF16)
    source = jnp.concatenate([bin_of, slot_of, valid, jnp.zeros((5, PAIR_PAD), F32)], axis=0)
    group_out[...] = dot(source.astype(BF16), to_group).astype(jnp.int32)
    taken = jnp.minimum(jnp.maximum(total - first, 0.0), room)
    bin_cols = jnp.concatenate([count, kept, first, taken, jnp.zeros((BINS, 124), F32)], axis=1)
    bin_out[...] = bin_cols.astype(jnp.int32)

    occ_row = iota((OCC, 1), 0).astype(F32)
    parts = split3(w_ref[...])
    rows = w_ref.shape[0]
    for k, w_out in enumerate((w_direct, w_mirror)):
        to_slot = jnp.where(columns[:, k : k + 1] == iota((PAIR_PAD, ALL_SLOTS), 1), 1.0, 0.0).astype(BF16)
        slots = dot(occ_ref[...].astype(BF16), to_slot)
        slot_i, slot_j, live = slots[0:1, :], slots[1:2, :], slots[2:3, :]
        if k == 0:
            wanted = slot_i * float(OCC) + slot_j
        else:
            wanted = slot_j * float(OCC) + slot_i
            energy = jnp.sum(
                jnp.where(slot_i == occ_row, eocc_ref[...], 0.0), axis=0, keepdims=True
            ) + jnp.sum(jnp.where(slot_j == occ_row, eocc_ref[...], 0.0), axis=0, keepdims=True)
            slot_out[...] = jnp.concatenate([energy, live, jnp.zeros((6, ALL_SLOTS), F32)], axis=0)
        wanted = jnp.where(live > 0.5, wanted, -1.0).astype(jnp.int32)
        w_out[...] = jnp.zeros(w_out.shape, F32)
        for lane in range(0, ALL_SLOTS, 128):
            wide = min(128, ALL_SLOTS - lane)
            pick = jnp.where(
                iota((OCC * OCC, wide), 0) == wanted[:, lane : lane + wide], 1.0, 0.0
            ).astype(BF16)
            w_out[0:rows, lane : lane + wide] = (dot(parts[0], pick) + dot(parts[1], pick)) + dot(
                parts[2], pick
            )


def prep(own, pair_group, e_occ, hole_ladder):
    pairs = pair_group.shape[0]
    first, second = np.triu_indices(OCC)
    occ = np.zeros((8, PAIR_PAD), np.float32)
    occ[0, :pairs], occ[1, :pairs], occ[2, :pairs] = first, second, 1.0
    group = jnp.pad(pair_group, (0, PAIR_PAD - pairs), constant_values=BINS).reshape(1, PAIR_PAD)
    vmem = pl.BlockSpec(memory_space=pltpu.VMEM)
    return pl.pallas_call(
        prep_kernel,
        out_shape=(
            jax.ShapeDtypeStruct((104, ALL_SLOTS), F32),
            jax.ShapeDtypeStruct((104, ALL_SLOTS), F32),
            jax.ShapeDtypeStruct((8, ALL_SLOTS), F32),
            jax.ShapeDtypeStruct((8, GROUP_SLOTS), jnp.int32),
            jax.ShapeDtypeStruct((BINS, 128), jnp.int32),
        ),
        in_specs=[pl.BlockSpec(memory_space=pltpu.SMEM)] + [vmem] * 4,
        out_specs=(vmem,) * 5,
        compiler_params=pltpu.CompilerParams(vmem_limit_bytes=VMEM_LIMIT),
    )(own, group, jnp.asarray(occ), e_occ.reshape(OCC, 1), hole_ladder)


def tile_kernel(t_ref, mirror_hi, mirror_lo, direct_hi, direct_lo):
    for h in range(2):
        for tile in range(5):
            for q in range(8):
                pieces = []
                for e in (2 * q, 2 * q + 1):
                    unit = 5 * tile + e // 3
                    if e < 15 and unit < 24:
                        pieces.append(t_ref[24 * h + unit, 8 * (e % 3) : 8 * (e % 3) + 8, :])
                    else:
                        pieces.append(jnp.zeros((8, 1600), F32))
                hi, lo = split2(jnp.concatenate(pieces, axis=0))
                at = 640 * h + 128 * tile + 16 * q
                mirror_hi[at : at + 16, :] = hi
                mirror_lo[at : at + 16, :] = lo
    for b in range(24):
        hi, lo = split2(t_ref[:, b, :])
        direct_hi[48 * b : 48 * (b + 1), :] = hi
        direct_lo[48 * b : 48 * (b + 1), :] = lo
    direct_hi[1152:1280, :] = jnp.zeros((128, 1600), BF16)
    direct_lo[1152:1280, :] = jnp.zeros((128, 1600), BF16)


def tile_parts(amplitudes):
    vmem = pl.BlockSpec(memory_space=pltpu.VMEM)
    return pl.pallas_call(
        tile_kernel,
        out_shape=(jax.ShapeDtypeStruct((1280, 1600), BF16),) * 4,
        in_specs=[vmem],
        out_specs=(vmem,) * 4,
        compiler_params=pltpu.CompilerParams(vmem_limit_bytes=VMEM_LIMIT),
        cost_estimate=pl.CostEstimate(flops=0, bytes_accessed=60_000_000, transcendentals=0),
    )(amplitudes)


def hole_kernel(mirror, w_ref, t_hi, t_lo, out_ref, wn, wt_hi, wt_lo):
    for s in range(16):
        wn[100 * s : 100 * s + 100, :] = w_ref[104 * s : 104 * s + 100, :]
    for lane in range(0, ALL_SLOTS, 128):
        wide = min(128, ALL_SLOTS - lane)
        hi, lo = split2(jnp.transpose(wn[:, lane : lane + wide], (1, 0)))
        wt_hi[lane : lane + wide, :] = hi
        wt_lo[lane : lane + wide, :] = lo

    for n in range(5):
        right_hi, right_lo = t_hi[256 * n : 256 * (n + 1), :], t_lo[256 * n : 256 * (n + 1), :]
        y = (dot_t(wt_lo[...], right_hi) + dot_t(wt_hi[...], right_lo)) + dot_t(wt_hi[...], right_hi)
        if mirror:
            for u in range(2):
                h, lane = divmod(2 * n + u, 5)
                first = 0
                for slots in (slice(HEAD, SLOTS), slice(0, HEAD)):
                    for b in range(BINS):
                        last = first + slots.stop - slots.start
                        out_ref[b, h, slots, 128 * lane : 128 * (lane + 1)] = y[
                            first:last, 128 * u : 128 * (u + 1)
                        ]
                        first = last
        else:
            wide = 256 if n < 4 else 128
            for b in range(BINS):
                out_ref[b, :, 256 * n : 256 * n + wide] = y[SLOTS * b : SLOTS * (b + 1), 0:wide]


def hole_product(mirror, gathered, hi, lo):
    shape = (BINS, 2, SLOTS, 640) if mirror else (BINS, SLOTS, 1152)
    vmem = pl.BlockSpec(memory_space=pltpu.VMEM)
    return pl.pallas_call(
        functools.partial(hole_kernel, mirror),
        out_shape=jax.ShapeDtypeStruct(shape, F32),
        in_specs=[vmem] * 3,
        out_specs=vmem,
        scratch_shapes=[
            pltpu.VMEM((1600, ALL_SLOTS), F32),
            pltpu.VMEM((ALL_SLOTS, 1600), BF16),
            pltpu.VMEM((ALL_SLOTS, 1600), BF16),
        ],
        compiler_params=pltpu.CompilerParams(vmem_limit_bytes=VMEM_LIMIT),
        cost_estimate=pl.CostEstimate(
            flops=2 * 3 * ALL_SLOTS * 1280 * 1600, bytes_accessed=17_000_000, transcendentals=0
        ),
    )(gathered, hi, lo)


def combine_kernel(head, size, *refs):
    if head:
        meta_ref, ed_ref, d_ref, s_ref, eo_ref, ev_ref, ladder_ref, tail_ref, flat_ref = refs[:9]
        new_ref, part_ref, m_ref, raw, acc = refs[9:]
    else:
        ed_ref, d_ref, s_ref, eo_ref, ev_ref, raw, m_ref = refs
    step = pl.program_id(0)
    energy = eo_ref[:, 0:1] - ev_ref[...]
    live = eo_ref[:, 1:2] > 0.5
    rows = slice(TAIL, SLOTS) if head else slice(0, TAIL)

    def group(j):
        for u in range(8):
            d = 8 * j + u
            direct = jnp.concatenate([d_ref[r, rows, 48 * u : 48 * (u + 1)] for r in range(8)], axis=1)
            lane = 128 * (d // 5) + 24 * (d % 5)
            mirrored = jnp.concatenate([s_ref[c, :, lane : lane + 24] for c in range(16)], axis=1)
            value = jnp.where(live, (direct + mirrored) / (energy - ed_ref[d]), 0.0)
            m_ref[0:size, 384 * u : 384 * (u + 1)] = value
            raw[:, u, :] = value

    for j in range(3):
        pl.when(step == j)(functools.partial(group, j))

    if not head:
        return
    kept = meta_ref[0]
    new_ref[0:size] = jnp.where(iota((size, 8, 384), 0) < kept, raw[...], 0.0)
    tail = iota((SLOTS - size, 8, 384), 0) + size
    new_ref[size:SLOTS] = jnp.where(tail < kept, tail_ref[...], 0.0)
    new_ref[SLOTS:] = jnp.zeros((new_ref.shape[0] - SLOTS, 8, 384), F32)

    m_ref[size:SLOTS, :] = flat_ref[...]
    left_hi, left_lo = split2(m_ref[...])
    right_hi, right_lo = split2(ladder_ref[...].reshape(8 * 384, 256))
    term = (dot(left_lo, right_hi) + dot(left_hi, right_lo)) + dot(left_hi, right_hi)

    @pl.when(step == 0)
    def _():
        acc[...] = jnp.zeros(acc.shape, F32)

    acc[0:SLOTS, :] += term

    @pl.when(step == 2)
    def _():
        part_ref[...] = jnp.transpose(acc[...], (1, 0))


def combine(size, ed, direct, mirrored, energy, ev, ladder, head=None, rows=0):
    smem = pl.BlockSpec(memory_space=pltpu.SMEM)
    in_specs = [
        smem,
        pl.BlockSpec((8, TAIL if head is None else SLOTS, 384), lambda j: (0, 0, j)),
        pl.BlockSpec((16, size, 640), lambda j: (0, 0, 0)),
        pl.BlockSpec((size, 2), lambda j: (0, 0)),
        pl.BlockSpec((1, 384), lambda j: (0, 0)),
    ]
    operands = [ed, direct, mirrored, energy, ev]
    scratch = []
    if head is None:
        out_shape = (jax.ShapeDtypeStruct((size, 24, 384), F32), jax.ShapeDtypeStruct((size, 24 * 384), F32))
        out_specs = (
            pl.BlockSpec((size, 8, 384), lambda j: (0, j, 0)),
            pl.BlockSpec((size, 8 * 384), lambda j: (0, j)),
        )
    else:
        meta, tail, flat = head
        operands = [meta] + operands + [ladder, tail, flat]
        in_specs = [smem] + in_specs + [
            pl.BlockSpec((8, 384, 256), lambda j: (j, 0, 0)),
            pl.BlockSpec((SLOTS - size, 8, 384), lambda j: (0, j, 0)),
            pl.BlockSpec((SLOTS - size, 8 * 384), lambda j: (0, j)),
        ]
        out_shape = (jax.ShapeDtypeStruct((rows, 24, 384), F32), jax.ShapeDtypeStruct((256, 128), F32))
        out_specs = (
            pl.BlockSpec((rows, 8, 384), lambda j: (0, j, 0)),
            pl.BlockSpec((256, 128), lambda j: (0, 0)),
        )
        scratch += [
            pltpu.VMEM((SLOTS, 8 * 384), F32),
            pltpu.VMEM((size, 8, 384), F32),
            pltpu.VMEM((128, 256), F32),
        ]
    return pl.pallas_call(
        functools.partial(combine_kernel, head is not None, size),
        grid=(3,),
        out_shape=out_shape,
        in_specs=in_specs,
        out_specs=out_specs,
        scratch_shapes=scratch,
        compiler_params=pltpu.CompilerParams(vmem_limit_bytes=VMEM_LIMIT),
        cost_estimate=pl.CostEstimate(
            flops=2 * 3 * 128 * 9216 * 256, bytes_accessed=40_000_000, transcendentals=0
        ),
    )(*operands)


def place_kernel(table_ref, new_ref, back_ref, out_ref, sem):
    rows = table_ref[2, 0]

    def send(k, carry):
        pltpu.make_async_copy(back_ref.at[table_ref[0, k]], out_ref.at[SLOTS + k], sem).start()
        return carry

    lax.fori_loop(0, rows, send, 0)

    def wait(k, carry):
        pltpu.make_async_copy(back_ref.at[0], out_ref.at[SLOTS], sem).wait()
        return carry

    lax.fori_loop(0, rows, wait, 0)


def place(table, new, back):
    hbm = pl.BlockSpec(memory_space=pl.ANY)
    vmem = pl.BlockSpec(memory_space=pltpu.VMEM)
    return pl.pallas_call(
        place_kernel,
        out_shape=jax.ShapeDtypeStruct(new.shape, F32),
        in_specs=[pl.BlockSpec(memory_space=pltpu.SMEM), hbm, vmem],
        out_specs=hbm,
        scratch_shapes=[pltpu.SemaphoreType.DMA],
        input_output_aliases={1: 0},
        compiler_params=pltpu.CompilerParams(vmem_limit_bytes=VMEM_LIMIT),
    )(table, new, back)


def nothing_kernel(x_ref, other_ref, out_ref):
    del x_ref, other_ref, out_ref


def after(x, other):
    hbm = pl.BlockSpec(memory_space=pl.ANY)
    return pl.pallas_call(
        nothing_kernel,
        out_shape=jax.ShapeDtypeStruct(x.shape, x.dtype),
        in_specs=[hbm, hbm],
        out_specs=hbm,
        input_output_aliases={0: 0},
    )(x, other)


def shards(amplitudes, hole_ladder, e_occ, e_vir, ladder_ints, pair_group):
    tile_cols = amplitudes.shape[1]
    capacity = 2 * pair_group.shape[0] // lax.axis_size("row")
    own = lax.axis_index("row")
    col_index = lax.axis_index("col")

    w_direct, w_mirror, slot_table, group_table, bin_table = prep(
        own.reshape(1), pair_group, e_occ, hole_ladder
    )
    w_direct = lax.all_gather(w_direct, "col", axis=0, tiled=True)
    w_mirror = lax.all_gather(w_mirror, "col", axis=0, tiled=True)
    mirror_hi, mirror_lo, direct_hi, direct_lo = tile_parts(amplitudes)

    direct = hole_product(False, w_direct, direct_hi, direct_lo)
    direct = lax.all_to_all(direct, "row", 0, 0)
    mirror = after(hole_product(True, w_mirror, mirror_hi, mirror_lo), direct)
    mirror = lax.all_to_all(mirror, "row", 0, 0).reshape(16, SLOTS, 640)
    tail_mirror = lax.all_to_all(mirror[:, HEAD:], "col", 0, 0)
    head_mirror = lax.all_to_all(after(mirror[:, :HEAD], tail_mirror), "col", 0, 0)

    def own_slots(first, size):
        return lax.dynamic_slice(slot_table, (0, first + own * size), (2, size)).T

    tail_energy, head_energy = own_slots(0, TAIL), own_slots(BINS * TAIL, HEAD)
    local_energy = lax.dynamic_slice_in_dim(e_vir, col_index * tile_cols, tile_cols)
    virtual = e_vir.reshape(1, -1)
    counts, kept, taken = bin_table[:, 0], bin_table[:, 1], bin_table[:, 3]
    own_count = lax.dynamic_index_in_dim(counts, own, 0, False)
    own_kept = jnp.minimum(own_count, SLOTS)
    start = jnp.minimum(kept, SLOTS - SPILL)
    own_start = lax.dynamic_index_in_dim(start, own, 0, False)
    fits = (jnp.max(taken) <= SPILL) & jnp.all((taken == 0) | (kept >= HEAD))

    late_rows, late_flat = combine(
        TAIL, local_energy, direct, tail_mirror, tail_energy, virtual, ladder_ints
    )
    segment = lax.dynamic_slice_in_dim(late_rows, jnp.maximum(own_start - HEAD, 0), SPILL, 0)
    back = lax.all_gather(segment, "row", axis=0, tiled=True)

    def whole(meta, direct, head_mirror, late_rows):
        return combine(
            HEAD, local_energy, direct, head_mirror, head_energy, virtual, ladder_ints,
            (meta, late_rows, late_flat), capacity,
        )

    new_rows, partial_value = whole(own_kept.reshape(1), direct, head_mirror, late_rows)

    blocks = lax.all_to_all(partial_value.reshape(16, 16, 128), "col", 0, 0)
    share = jnp.sum(blocks, axis=0)
    shares = lax.all_to_all(jnp.broadcast_to(share, (BINS, 16, 128)), "row", 0, 0)
    live = group_table[2, :capacity]
    from_bin, from_slot = group_table[0, :capacity], group_table[1, :capacity]
    where_from = jnp.where(live > 0, from_bin * 128 + from_slot, -1)
    pick = jnp.arange(BINS * 128, dtype=jnp.int32)[:, None] == where_from[None, :]
    ladder_share = jnp.dot(
        jnp.transpose(shares, (1, 0, 2)).reshape(16, BINS * 128),
        pick.astype(F32),
        precision=lax.Precision.HIGHEST,
        preferred_element_type=F32,
    )

    late_bin, late_slot = from_bin[SLOTS:], from_slot[SLOTS:]
    late_count = own_count - own_kept
    bin_start = jnp.sum(jnp.where(late_bin[:, None] == jnp.arange(BINS)[None, :], start[None, :], 0), axis=1)
    back_row = jnp.clip(late_bin * SPILL + late_slot - bin_start, 0, BINS * SPILL - 1)
    count_row = jnp.full_like(back_row, jnp.where(fits, late_count, 0))
    new_amps = place(jnp.stack([back_row, back_row, count_row]), new_rows, back)

    def long_way(carry):
        turn, new_amps, direct, head_mirror, late_rows = carry
        values, _ = whole(jnp.full((1,), SLOTS, jnp.int32) + turn, direct, head_mirror, late_rows)
        everything = lax.all_gather(values[:SLOTS], "row", axis=0, tiled=True)
        late = everything[late_bin * SLOTS + late_slot]
        rows = jnp.arange(capacity - SLOTS, dtype=jnp.int32)
        table = jnp.stack([rows, rows, jnp.full_like(rows, late_count)])
        return turn + 1, place(table, new_amps, late), direct, head_mirror, late_rows

    turns = jnp.where(fits, 0, 1)
    new_amps = lax.while_loop(
        lambda carry: carry[0] < turns, long_way, (jnp.int32(0), new_amps, direct, head_mirror, late_rows)
    )[1]
    return (new_amps[None], ladder_share[None])


def solution(mesh):
    return jax.shard_map(
        shards,
        mesh=mesh,
        in_specs=(P("row", "col", None), P("col", None), P(), P(), P("col", None, None), P()),
        out_specs=(P("row", None, "col", None), P("row", "col", None)),
        check_vma=False,
    )
```
